512 devices in a mesh: batch: 64 (over y, z), tensor: 8 (over x, core).
Axes of the slice: x: 4, y: 4, z: 16, core: 2. Of those that a mesh axis runs over, the one named last changes fastest.
Arguments:
- tokens: bfloat16 [8192, 8192], P('batch', 'tensor'), may hold values from -6 to 6
- cotangent: bfloat16 [8192, 8192], P('batch', 'tensor'), may hold values from -1.5 to 1.5
- game_ids: int32 [8192], P('batch'), may hold values from 0 to 31, as said below
- adapters: bfloat16 [64, 8192, 1024], P('batch', 'tensor'), may hold values from -0.1875 to 0.1875
Outputs:
- input_grad: bfloat16 [8192, 8192], P('batch', 'tensor')
- adapter_grad: bfloat16 [64, 8192, 1024], P('batch', 'tensor')
The draws below stay inside these ranges and needn't reach their ends.
Inputs may be any that keep to these rules, and one draw needn't show every extreme that they name: `game_ids`: among the 128 tokens of each batch index no game appears more than 8 times; one game, the same for every batch index, appears exactly 8 times at every batch index.
All inputs are finite; a program needn't handle non-finite values.
Results may differ from the reference program's by a relative error of at most 0.0056.
Values may be sent and summed in bfloat16 or wider, within the bound.
A program may use at most 64 MiB of HBM per device.

```python
import jax
import jax.numpy as jnp
from jax import lax

D = 8192
HID = 1024
TOK_DEV = 128
GAMES = 32
CAP = 8
TOKENS = 8192
N_BATCH = 64


def draw_game_ids(key, part):
    key = jax.random.fold_in(key, 11)
    hot_key, rest_key = jax.random.split(key)
    block_count = TOKENS // TOK_DEV
    hot_game = jax.random.randint(hot_key, (), 0, GAMES).astype(jnp.int32)

    def one_block(block_key):
        slot_key, order_key = jax.random.split(block_key)
        chosen = jax.random.permutation(slot_key, (GAMES - 1) * CAP)[:TOK_DEV - CAP]
        other_games = (chosen // CAP).astype(jnp.int32)
        other_games = other_games + (other_games >= hot_game).astype(jnp.int32)
        block_games = jnp.concatenate([jnp.zeros((CAP,), jnp.int32) + hot_game, other_games])
        return block_games[jax.random.permutation(order_key, TOK_DEV)]
    block_keys = jax.random.split(rest_key, block_count)
    return jax.vmap(one_block)(block_keys).reshape(TOKENS).astype(jnp.int32)


def shard_levels(rng, extent, pieces, least, top_value):
    factor_of, own = 1.0, jax.random.fold_in(rng, 6)
    for axis_at, parts in pieces:
        heights = jnp.exp(jax.random.uniform(jax.random.fold_in(own, axis_at), (parts,), jnp.float32, least / len(pieces), top_value / len(pieces)))
        factor_of = factor_of * jnp.repeat(heights, extent[axis_at] // parts).reshape([-1 if axis == axis_at else 1 for axis in range(len(extent))])
    return factor_of


def gaussian(stream_key, shape, deviation, limit, cuts=(), kind=jnp.bfloat16):
    gain = shard_levels(stream_key, shape, cuts, -0.22, 0.18) if cuts else 1.0
    entries = jax.random.normal(stream_key, shape, jnp.float32) * deviation * gain
    return jnp.minimum(jnp.maximum(entries, -limit), limit).astype(kind)


def setup_inputs(seed: int = 0) -> dict:
    keys = jax.random.split(jax.random.key(seed), 5)
    tokens = gaussian(keys[0], (TOKENS, D), 1.0, 6.0, ((0, 64), (1, 8)))
    cotangent = gaussian(keys[1], (TOKENS, D), 0.25, 1.5, ((0, 64), (1, 8)))
    game_ids = draw_game_ids(jax.random.fold_in(keys[4], 71), 0)
    adapters = gaussian(keys[3], (2 * GAMES, D, HID), HID ** -0.5, 0.1875, ((0, 64), (1, 8)))
    return {"tokens": tokens, "cotangent": cotangent, "game_ids": game_ids, "adapters": adapters}


GELU_SCALE = 0.7978845608028654
GELU_CUBIC = 0.044715


def smooth_gate(values_in):
    inner_arg = GELU_SCALE * (values_in + GELU_CUBIC * values_in * values_in * values_in)
    return 0.5 * values_in * (1.0 + jnp.tanh(inner_arg))


def gate_slope(values_in):
    inner_arg = GELU_SCALE * (values_in + GELU_CUBIC * values_in * values_in * values_in)
    tangent = jnp.tanh(inner_arg)
    return 0.5 * (1.0 + tangent) + 0.5 * values_in * (1.0 - tangent * tangent) * GELU_SCALE * (1.0 + 3.0 * GELU_CUBIC * values_in * values_in)


def reference(tokens, cotangent, game_ids, adapters):
    rows_max = N_BATCH * CAP
    zero_row = jnp.zeros((1, D), jnp.bfloat16)
    padded_tokens = jnp.concatenate([tokens, zero_row], axis=0)
    padded_grads = jnp.concatenate([cotangent, zero_row], axis=0)
    contract_rows = (((0,), (0,)), ((), ()))
    contract_cols = (((1,), (1,)), ((), ()))

    def per_game(carry_back, game_id):
        row_index = jnp.nonzero(game_ids == game_id, size=rows_max, fill_value=TOKENS)[0].astype(jnp.int32)
        inputs = jnp.take(padded_tokens, row_index, axis=0)
        upstream = jnp.take(padded_grads, row_index, axis=0)
        w_in = lax.dynamic_index_in_dim(adapters, 2 * game_id, 0, keepdims=False)
        w_out_t = lax.dynamic_index_in_dim(adapters, 2 * game_id + 1, 0, keepdims=False)
        pre_act = jnp.dot(inputs, w_in, preferred_element_type=jnp.float32)
        hidden = smooth_gate(pre_act).astype(jnp.bfloat16)
        back_hidden = jnp.dot(upstream, w_out_t, preferred_element_type=jnp.float32).astype(jnp.bfloat16)
        delta_rows = (back_hidden.astype(jnp.float32) * gate_slope(pre_act)).astype(jnp.bfloat16)
        grad_in = lax.dot_general(inputs, delta_rows, contract_rows, preferred_element_type=jnp.float32).astype(jnp.bfloat16)
        grad_out = lax.dot_general(upstream, hidden, contract_rows, preferred_element_type=jnp.float32).astype(jnp.bfloat16)
        back_rows = lax.dot_general(delta_rows, w_in, contract_cols, preferred_element_type=jnp.float32).astype(jnp.bfloat16)
        carry_back = carry_back.at[row_index].set(back_rows)
        return carry_back, jnp.stack([grad_in, grad_out])

    start_back = jnp.zeros((TOKENS + 1, D), jnp.bfloat16)
    final_back, grad_pairs = lax.scan(per_game, start_back, jnp.arange(GAMES, dtype=jnp.int32))
    return final_back[:TOKENS], grad_pairs.reshape(2 * GAMES, D, HID)
```

```python
import functools

import jax
import jax.numpy as jnp
from jax import lax
from jax.experimental import pallas as pl
from jax.experimental.pallas import tpu as pltpu
from jax.sharding import PartitionSpec as P

MESH = pl.DeviceIdType.MESH
GELU_SCALE = 0.7978845608028654
GELU_CUBIC = 0.044715
CAP = 8
NY = 4
F32 = jnp.float32
BF16 = jnp.bfloat16


def smooth_gate(v):
    inner = GELU_SCALE * (v + GELU_CUBIC * v * v * v)
    return 0.5 * v * (1.0 + jnp.tanh(inner))


def gate_slope(v):
    inner = GELU_SCALE * (v + GELU_CUBIC * v * v * v)
    tangent = jnp.tanh(inner)
    return 0.5 * (1.0 + tangent) + 0.5 * v * (1.0 - tangent * tangent) * GELU_SCALE * (
        1.0 + 3.0 * GELU_CUBIC * v * v
    )


def kernel(
    ny, nz, nt, part_type,
    ids_ref, tok_hbm, cot_hbm, w_hbm,
    ig_hbm, ag_hbm,
    tok, cot, w, sends, arrived, rows, part, summands, swap_out, swap_in, mixed, bsend, back, ig, ag,
    in_sem, out_sem, self_sem, fwd_send, fwd_recv, rs_send, rs_recv, swap_send, swap_recv, ag_send, ag_recv,
    back_send, back_recv,
):
    nb = ny * nz
    np_ = nz // 2
    me = lax.axis_index("batch")
    t = lax.axis_index("tensor")
    y, z = me // nz, me % nz
    p, par = z // 2, z % 2
    count, features = tok.shape
    hidden = w.shape[1]
    half = features // 2
    games = nb // 2
    chunk = nz * CAP
    piece = chunk // nt

    copies = [
        pltpu.make_async_copy(a, b, in_sem.at[i])
        for i, (a, b) in enumerate(((tok_hbm, tok), (cot_hbm, cot), (w_hbm, w)))
    ]
    for c in copies:
        c.start()

    barrier = pltpu.get_barrier_semaphore()

    def greet_batch(k, _):
        pl.semaphore_signal(barrier, inc=1, device_id={"batch": (me + k) % nb}, device_id_type=MESH)
        return _

    def greet_tensor(k, _):
        pl.semaphore_signal(barrier, inc=1, device_id={"tensor": (t + k) % nt}, device_id_type=MESH)
        return _

    lax.fori_loop(1, nb, greet_batch, 0)
    lax.fori_loop(1, nt, greet_tensor, 0)

    ids = ids_ref[...]
    member = (lax.broadcasted_iota(jnp.int32, (games, count), 0) == ids).astype(F32)
    earlier = (
        lax.broadcasted_iota(jnp.int32, (count, count), 0) < lax.broadcasted_iota(jnp.int32, (count, count), 1)
    ).astype(F32)
    before = jnp.dot(member.astype(BF16), earlier.astype(BF16), preferred_element_type=F32)
    position = jnp.sum(before * member, axis=0, keepdims=True).astype(jnp.int32)
    gy, gp = ids // np_, ids % np_
    target = (((gy - y + ny) % ny) * np_ + (gp - p + np_) % np_) * CAP + position

    place = lax.broadcasted_iota(jnp.int32, (2 * games * CAP, count), 0)
    slot = (place // 16) * CAP + place % CAP
    placing = (slot == target).astype(BF16)
    on_left = lax.broadcasted_iota(jnp.int32, (2 * games * CAP, half), 0) % 16 < 8
    for q in range(2):
        copies[q].wait()
        src = (tok, cot)[q]
        left = jnp.dot(placing, src[:, :half], preferred_element_type=F32)
        right = jnp.dot(placing, src[:, half:], preferred_element_type=F32)
        sends[q] = jnp.where(on_left, left, right).astype(BF16).reshape(games, 16, half)

    pl.semaphore_wait(barrier, nb - 1 + nt - 1)

    own_block = pltpu.make_async_copy(sends.at[par, 0], arrived.at[0, par], self_sem.at[0])
    own_block.start()

    def send_forward(j, _):
        dy, r = j // np_, j % np_
        dp = (np_ // 2 + (r % 2) * (r + 1) // 2 - ((r + 1) % 2) * (r // 2) + np_) % np_
        far_y = (y + dy) % ny
        far_p = (p + dp) % np_
        for q in range(2):
            far = far_y * nz + 2 * far_p + q

            @pl.when(far != me)
            def _send():
                pltpu.make_async_remote_copy(
                    src_ref=sends.at[q, dy * np_ + dp],
                    dst_ref=arrived.at[dy, 2 * dp + par],
                    send_sem=fwd_send,
                    recv_sem=fwd_recv.at[dy],
                    device_id={"batch": far},
                    device_id_type=MESH,
                ).start()

        return _

    lax.fori_loop(0, ny * np_, send_forward, 0)
    copies[2].wait()

    tile = min(256, hidden)

    def per_chunk(c, _):
        @pl.when(c == 0)
        def _first():
            own_block.wait()
            ref = arrived.at[0, pl.ds(0, nz - 1)]
            pltpu.make_async_copy(ref, ref, fwd_recv.at[0]).wait()

        @pl.when(c != 0)
        def _later():
            ref = arrived.at[c]
            pltpu.make_async_copy(ref, ref, fwd_recv.at[c]).wait()

        wide = arrived[c].astype(F32).reshape(nz, 2, CAP, half)
        rows[c, :, :half] = wide[:, 0].reshape(chunk, half).astype(BF16)
        rows[c, :, half:] = wide[:, 1].reshape(chunk, half).astype(BF16)

        def times_w(j, _):
            cols = pl.ds(pl.multiple_of(j * tile, tile), tile)
            product = jnp.dot(rows[c], w[:, cols], preferred_element_type=F32)
            part[c, :, :, cols] = product.reshape(nt, piece, tile).astype(part_type)
            return _

        lax.fori_loop(0, hidden // tile, times_w, 0)

        def send_part(k, _):
            far = (t + k) % nt
            pltpu.make_async_remote_copy(
                src_ref=part.at[c, far],
                dst_ref=summands.at[c, k - 1],
                send_sem=rs_send,
                recv_sem=rs_recv.at[c],
                device_id={"tensor": far},
                device_id_type=MESH,
            ).start()
            return _

        lax.fori_loop(1, nt, send_part, 0)
        ref = summands.at[c]
        pltpu.make_async_copy(ref, ref, rs_recv.at[c]).wait()
        total = part[c, t].astype(F32)
        for k in range(nt - 1):
            total = total + summands[c, k].astype(F32)
        swap_out[c] = jnp.where(par == 0, smooth_gate(total), total).astype(BF16)
        swap = pltpu.make_async_remote_copy(
            src_ref=swap_out.at[c],
            dst_ref=swap_in.at[c],
            send_sem=swap_send,
            recv_sem=swap_recv.at[c],
            device_id={"batch": me + 1 - 2 * par},
            device_id_type=MESH,
        )
        swap.start()
        slope = jnp.where(par == 0, gate_slope(total), 1.0)
        swap.wait_recv()
        mixed[c, t] = (swap_in[c].astype(F32) * slope).astype(BF16)

        def send_mixed(k, _):
            pltpu.make_async_remote_copy(
                src_ref=mixed.at[c, t],
                dst_ref=mixed.at[c, t],
                send_sem=ag_send,
                recv_sem=ag_recv.at[c],
                device_id={"tensor": (t + k) % nt},
                device_id_type=MESH,
            ).start()
            return _

        lax.fori_loop(1, nt, send_mixed, 0)
        ref = mixed.at[c, pl.ds(0, nt - 1)]
        pltpu.make_async_copy(ref, ref, ag_recv.at[c]).wait()

        @pl.when(par == 0)
        def _input_gradient():
            grad = lax.dot_general(
                mixed[c].reshape(chunk, hidden), w[...], (((1,), (1,)), ((), ())), preferred_element_type=F32
            )
            pair = jnp.stack(
                [grad[:, :half].reshape(nz, CAP, half), grad[:, half:].reshape(nz, CAP, half)], axis=1
            )
            bsend[c] = pair.reshape(nz, 16, half).astype(BF16)

            def send_back(j, _):
                dp, from_par = j // 2, j % 2
                far = ((y - c + ny) % ny) * nz + 2 * ((p - dp + np_) % np_) + from_par

                @pl.when(far != me)
                def _send():
                    pltpu.make_async_remote_copy(
                        src_ref=bsend.at[c, j],
                        dst_ref=back.at[c * np_ + dp],
                        send_sem=back_send,
                        recv_sem=back_recv,
                        device_id={"batch": far},
                        device_id_type=MESH,
                    ).start()

                @pl.when(far == me)
                def _keep():
                    pltpu.make_async_copy(bsend.at[0, 0], back.at[0], self_sem.at[1]).start()

                return _

            lax.fori_loop(0, nz, send_back, 0)

        return _

    lax.fori_loop(0, ny, per_chunk, 0)

    every = ny * chunk

    def adapter_columns(j, _):
        cols = pl.ds(pl.multiple_of(j * tile, tile), tile)
        product = lax.dot_general(
            rows[...].reshape(every, features), mixed[:, :, :, cols].reshape(every, tile), (((0,), (0,)), ((), ())),
            preferred_element_type=F32,
        )
        ag[:, cols] = product.astype(BF16)
        return _

    lax.fori_loop(0, hidden // tile, adapter_columns, 0)
    ag_copy = pltpu.make_async_copy(ag, ag_hbm, out_sem.at[0])
    ag_copy.start()

    eye = lax.broadcasted_iota(jnp.int32, (count, count), 0) == lax.broadcasted_iota(jnp.int32, (count, count), 1)
    target_column = jnp.sum(jnp.where(eye, target, 0), axis=1, keepdims=True)
    taking = (lax.broadcasted_iota(jnp.int32, (count, games * CAP), 1) == target_column).astype(BF16)

    @pl.when(par == 0)
    def _with_own():
        pltpu.make_async_copy(bsend.at[0, 0], back.at[0], self_sem.at[1]).wait()
        ref = back.at[pl.ds(0, games - 1)]
        pltpu.make_async_copy(ref, ref, back_recv).wait()

    @pl.when(par != 0)
    def _without_own():
        pltpu.make_async_copy(back, back, back_recv).wait()

    wide = back[...].astype(F32).reshape(games, 2, CAP, half)
    for h in range(2):
        side = wide[:, h].reshape(games * CAP, half).astype(BF16)
        ig[:, h * half:(h + 1) * half] = jnp.dot(taking, side, preferred_element_type=F32).astype(BF16)
    ig_copy = pltpu.make_async_copy(ig, ig_hbm, out_sem.at[1])
    ig_copy.start()

    ref = sends.at[:, pl.ds(0, games - 1)]
    pltpu.make_async_copy(ref, ref, fwd_send).wait()
    ref = sends.at[0, 0]
    pltpu.make_async_copy(ref, ref, fwd_send).wait()
    ref = summands
    pltpu.make_async_copy(ref, ref, rs_send).wait()
    pltpu.make_async_copy(swap_out, swap_out, swap_send).wait()
    ref = mixed.at[:, pl.ds(0, nt - 1)]
    pltpu.make_async_copy(ref, ref, ag_send).wait()

    @pl.when(par == 0)
    def _sent_back():
        for ref in (bsend.at[pl.ds(0, ny - 1)], bsend.at[0, pl.ds(0, nz - 1)]):
            pltpu.make_async_copy(ref, ref, back_send).wait()

    ag_copy.wait()
    ig_copy.wait()


def solution(mesh, ny=NY, part_type=BF16, interpret=False):
    nb, nt = mesh.shape["batch"], mesh.shape["tensor"]
    nz = nb // ny

    def body(tokens, cotangent, game_ids, adapters):
        count, features = tokens.shape
        hidden = adapters.shape[2]
        games = nb // 2
        half = features // 2
        chunk = nz * CAP
        piece = chunk // nt
        dma = pltpu.SemaphoreType.DMA
        any_ = pl.BlockSpec(memory_space=pl.ANY)
        ig, ag = pl.pallas_call(
            functools.partial(kernel, ny, nz, nt, part_type),
            out_shape=(
                jax.ShapeDtypeStruct((count, features), BF16),
                jax.ShapeDtypeStruct((features, hidden), BF16),
            ),
            in_specs=[pl.BlockSpec(memory_space=pltpu.VMEM), any_, any_, any_],
            out_specs=(any_, any_),
            scratch_shapes=[
                pltpu.VMEM((count, features), BF16),
                pltpu.VMEM((count, features), BF16),
                pltpu.VMEM((features, hidden), BF16),
                pltpu.VMEM((2, games, 16, half), BF16),
                pltpu.VMEM((ny, nz, 16, half), BF16),
                pltpu.VMEM((ny, chunk, features), BF16),
                pltpu.VMEM((ny, nt, piece, hidden), part_type),
                pltpu.VMEM((ny, nt - 1, piece, hidden), part_type),
                pltpu.VMEM((ny, piece, hidden), BF16),
                pltpu.VMEM((ny, piece, hidden), BF16),
                pltpu.VMEM((ny, nt, piece, hidden), BF16),
                pltpu.VMEM((ny, nz, 16, half), BF16),
                pltpu.VMEM((games, 16, half), BF16),
                pltpu.VMEM((count, features), BF16),
                pltpu.VMEM((features, hidden), BF16),
                dma((3,)), dma((2,)), dma((2,)),
                dma, dma((ny,)),
                dma, dma((ny,)),
                dma, dma((ny,)),
                dma, dma((ny,)),
                dma, dma,
            ],
            compiler_params=pltpu.CompilerParams(
                collective_id=0, has_side_effects=True, vmem_limit_bytes=48 << 20
            ),
            interpret=interpret,
        )(game_ids.reshape(1, count), tokens, cotangent, adapters.reshape(features, hidden))
        return ig, ag.reshape(1, features, hidden)

    return jax.shard_map(
        body,
        mesh=mesh,
        in_specs=(P("batch", "tensor"), P("batch", "tensor"), P("batch"), P("batch", "tensor", None)),
        out_specs=(P("batch", "tensor"), P("batch", "tensor", None)),
        check_vma=False,
    )
```

```python
import functools

import jax
import jax.numpy as jnp
from jax import lax
from jax.experimental import pallas as pl
from jax.experimental.pallas import tpu as pltpu
from jax.sharding import PartitionSpec as P

MESH = pl.DeviceIdType.MESH
GELU_SCALE = 0.7978845608028654
GELU_CUBIC = 0.044715
CAP = 8
AHEAD = 2
NY = 4
F32 = jnp.float32
BF16 = jnp.bfloat16


def smooth_gate(v):
    inner = GELU_SCALE * (v + GELU_CUBIC * v * v * v)
    return 0.5 * v * (1.0 + jnp.tanh(inner))


def gate_slope(v):
    inner = GELU_SCALE * (v + GELU_CUBIC * v * v * v)
    tangent = jnp.tanh(inner)
    return 0.5 * (1.0 + tangent) + 0.5 * v * (1.0 - tangent * tangent) * GELU_SCALE * (
        1.0 + 3.0 * GELU_CUBIC * v * v
    )


def kernel(
    ny, nz, nt, part_type,
    ids_ref, tok_hbm, cot_hbm, w_hbm,
    ig_hbm, ag_hbm,
    tok, cot, w, sends, relay, arrived, rows, part, summands, swap_out, swap_in, slope, mixed, bsend, back, ig, ag,
    in_sem, out_sem, self_sem, relay_send, relay_recv, fwd_send, fwd_recv, rs_send, rs_recv, swap_send, swap_recv, ag_send, ag_recv,
    back_send, back_recv,
):
    nb = ny * nz
    np_ = nz // 2
    me = lax.axis_index("batch")
    t = lax.axis_index("tensor")
    y, z = me // nz, me % nz
    p, par = z // 2, z % 2
    core, x = t % 2, t // 2
    sibling = t + 1 - 2 * core
    gather_core = 1 - par
    gathers = core == gather_core
    count, features = tok.shape
    hidden = w.shape[1]
    half = features // 2
    games = nb // 2
    chunk = nz * CAP
    pieces = nt // 2
    piece = chunk // pieces
    up = np_ // 2

    copies = [
        pltpu.make_async_copy(a, b, in_sem.at[i])
        for i, (a, b) in enumerate(((tok_hbm, tok), (cot_hbm, cot), (w_hbm, w)))
    ]
    for c in copies:
        c.start()

    barrier = pltpu.get_barrier_semaphore()

    def greet_batch(k, _):
        pl.semaphore_signal(barrier, inc=1, device_id={"batch": (me + k) % nb}, device_id_type=MESH)
        return _

    def greet_tensor(k, _):
        pl.semaphore_signal(barrier, inc=1, device_id={"tensor": (t + k) % nt}, device_id_type=MESH)
        return _

    lax.fori_loop(1, nb, greet_batch, 0)
    lax.fori_loop(1, nt, greet_tensor, 0)

    ids = ids_ref[...]
    member = (lax.broadcasted_iota(jnp.int32, (games, count), 0) == ids).astype(F32)
    earlier = (
        lax.broadcasted_iota(jnp.int32, (count, count), 0) < lax.broadcasted_iota(jnp.int32, (count, count), 1)
    ).astype(F32)
    before = jnp.dot(member.astype(BF16), earlier.astype(BF16), preferred_element_type=F32)
    position = jnp.sum(before * member, axis=0, keepdims=True).astype(jnp.int32)
    gy, gp = ids // np_, ids % np_
    target = (((gy - y + ny) % ny) * np_ + (gp - p + np_) % np_) * CAP + position

    place = lax.broadcasted_iota(jnp.int32, (2 * games * CAP, count), 0)
    slot = (place // 16) * CAP + place % CAP
    placing = (slot == target).astype(BF16)
    on_left = lax.broadcasted_iota(jnp.int32, (2 * games * CAP, half), 0) % 16 < 8
    for q in range(2):
        copies[q].wait()
        src = (tok, cot)[q]
        left = jnp.dot(placing, src[:, :half], preferred_element_type=F32)
        right = jnp.dot(placing, src[:, half:], preferred_element_type=F32)
        sends[:, q] = jnp.where(on_left, left, right).astype(BF16).reshape(games, 16, half)

    pl.semaphore_wait(barrier, nb - 1 + nt - 1)

    own_block = pltpu.make_async_copy(sends.at[0, par], arrived.at[0, par], self_sem.at[0])
    own_block.start()

    def relay_part(dy, for_core):
        first, number = ((1, up), (up + 1, up - 1))[for_core]
        return sends.at[pl.ds(dy * np_ + first, number)], relay.at[dy, pl.ds(0, number)]

    for c in range(2):

        @pl.when(core != c)
        def _hand_over():
            def hand_over(dy, _):
                src, dst = relay_part(dy, c)
                pltpu.make_async_remote_copy(
                    src_ref=src,
                    dst_ref=dst,
                    send_sem=relay_send,
                    recv_sem=relay_recv.at[dy],
                    device_id={"tensor": sibling},
                    device_id_type=MESH,
                ).start()
                return _

            lax.fori_loop(0, ny, hand_over, 0)

    def send_block(src, dy, dp, q, tensor):
        far = ((y + dy) % ny) * nz + 2 * ((p + dp) % np_) + q
        pltpu.make_async_remote_copy(
            src_ref=src,
            dst_ref=arrived.at[dy, 2 * dp + par],
            send_sem=fwd_send,
            recv_sem=fwd_recv.at[dy],
            device_id={"batch": far, "tensor": tensor},
            device_id_type=MESH,
        ).start()

    def send_forward(dy, _):
        for c in range(2):

            @pl.when(core == c)
            def _own_way():
                number = up - c

                def own(i, _):
                    dp = up + 1 + i if c else up - i
                    for q in range(2):
                        send_block(sends.at[dy * np_ + dp, q], dy, dp, q, t)
                    return _

                def relayed(i, _):
                    dp = up + 1 + i if c else up - i
                    for q in range(2):
                        send_block(relay.at[dy, i if c else up - 1 - i, q], dy, dp, q, sibling)
                    return _

                lax.fori_loop(0, number, own, 0)
                _, ref = relay_part(dy, c)
                pltpu.make_async_copy(ref, ref, relay_recv.at[dy]).wait()
                lax.fori_loop(0, number, relayed, 0)

        send_block(sends.at[dy * np_, 1 - par], dy, 0, 1 - par, t)

        @pl.when(dy != 0)
        def _straight():
            send_block(sends.at[dy * np_, par], dy, 0, par, t)

        return _

    lax.fori_loop(0, AHEAD, send_forward, 0)
    copies[2].wait()

    def arrive(c):
        @pl.when(c == 0)
        def _first():
            own_block.wait()
            ref = arrived.at[0, pl.ds(0, nz - 1)]
            pltpu.make_async_copy(ref, ref, fwd_recv.at[0]).wait()

        @pl.when(c != 0)
        def _later():
            ref = arrived.at[c]
            pltpu.make_async_copy(ref, ref, fwd_recv.at[c]).wait()

        @pl.when(c + AHEAD < ny)
        def _next():
            send_forward(c + AHEAD, 0)

        wide = arrived[c].astype(F32).reshape(nz, 2, CAP, half)
        rows[c, :, :half] = wide[:, 0].reshape(chunk, half).astype(BF16)
        rows[c, :, half:] = wide[:, 1].reshape(chunk, half).astype(BF16)

        product = jnp.dot(rows[c], w[...], preferred_element_type=F32)
        part[c] = product.reshape(pieces, piece, hidden).astype(part_type)

        def send_part(k, _):
            to = (x + k) % pieces

            @pl.when(2 * to + gather_core != t)
            def _send():
                far = 2 * to + gather_core
                pltpu.make_async_remote_copy(
                    src_ref=part.at[c, to],
                    dst_ref=summands.at[c, (t - far + nt) % nt - 1],
                    send_sem=rs_send,
                    recv_sem=rs_recv.at[c],
                    device_id={"tensor": far},
                    device_id_type=MESH,
                ).start()

            return _

        lax.fori_loop(0, pieces, send_part, 0)

    def swap_copy(c):
        return pltpu.make_async_remote_copy(
            src_ref=swap_out.at[c],
            dst_ref=swap_in.at[c],
            send_sem=swap_send,
            recv_sem=swap_recv.at[c],
            device_id={"batch": me + 1 - 2 * par, "tensor": 2 * x + par},
            device_id_type=MESH,
        )

    def combine(c):
        ref = summands.at[c]
        pltpu.make_async_copy(ref, ref, rs_recv.at[c]).wait()
        total = part[c, x].astype(F32)
        for k in range(nt - 1):
            total = total + summands[c, k].astype(F32)
        swap_out[c] = jnp.where(par == 0, smooth_gate(total), total).astype(BF16)
        swap_copy(c).start()
        slope[...] = jnp.where(par == 0, gate_slope(total), 1.0)

    def spread(c):
        swap_copy(c).wait_recv()
        mixed[c, x] = (swap_in[c].astype(F32) * slope[...]).astype(BF16)

        def send_mixed(k, _):
            pltpu.make_async_remote_copy(
                src_ref=mixed.at[c, x],
                dst_ref=mixed.at[c, x],
                send_sem=ag_send,
                recv_sem=ag_recv.at[c],
                device_id={"tensor": (t + k) % nt},
                device_id_type=MESH,
            ).start()
            return _

        lax.fori_loop(1, nt, send_mixed, 0)

    def give_back(c):
        for number, yes in ((pieces - 1, gathers), (pieces, jnp.logical_not(gathers))):
            if number > 0:

                @pl.when(yes)
                def _wait():
                    ref = mixed.at[c, pl.ds(0, number)]
                    pltpu.make_async_copy(ref, ref, ag_recv.at[c]).wait()

        @pl.when(par == 0)
        def _input_gradient():
            grad = lax.dot_general(
                mixed[c].reshape(chunk, hidden), w[...], (((1,), (1,)), ((), ())), preferred_element_type=F32
            )
            pair = jnp.stack(
                [grad[:, :half].reshape(nz, CAP, half), grad[:, half:].reshape(nz, CAP, half)], axis=1
            )
            bsend[c] = pair.reshape(nz, 16, half).astype(BF16)

    def start_back(c):
        @pl.when(par == 0)
        def _start():
            def send_back(j, _):
                dp, from_par = j // 2, j % 2
                far = ((y - c + ny) % ny) * nz + 2 * ((p - dp + np_) % np_) + from_par

                @pl.when(far != me)
                def _send():
                    pltpu.make_async_remote_copy(
                        src_ref=bsend.at[c, j],
                        dst_ref=back.at[c * np_ + dp],
                        send_sem=back_send,
                        recv_sem=back_recv,
                        device_id={"batch": far},
                        device_id_type=MESH,
                    ).start()

                @pl.when(far == me)
                def _keep():
                    pltpu.make_async_copy(bsend.at[0, 0], back.at[0], self_sem.at[1]).start()

                return _

            lax.fori_loop(0, nz, send_back, 0)

    def per_chunk(k, _):
        @pl.when(k < ny)
        def _arrive():
            arrive(k)

        @pl.when(k > 0)
        def _give_back():
            give_back(k - 1)

        @pl.when((k < ny) & gathers)
        def _combine():
            combine(k)

        @pl.when(k > 0)
        def _start_back():
            start_back(k - 1)

        @pl.when((k < ny) & gathers)
        def _spread():
            spread(k)

        return _

    lax.fori_loop(0, ny + 1, per_chunk, 0)

    every = ny * chunk

    product = lax.dot_general(
        rows[...].reshape(every, features), mixed[...].reshape(every, hidden), (((0,), (0,)), ((), ())),
        preferred_element_type=F32,
    )
    ag[...] = product.astype(BF16)
    ag_copy = pltpu.make_async_copy(ag, ag_hbm, out_sem.at[0])
    ag_copy.start()

    eye = lax.broadcasted_iota(jnp.int32, (count, count), 0) == lax.broadcasted_iota(jnp.int32, (count, count), 1)
    target_column = jnp.sum(jnp.where(eye, target, 0), axis=1, keepdims=True)
    taking = (lax.broadcasted_iota(jnp.int32, (count, games * CAP), 1) == target_column).astype(BF16)

    @pl.when(par == 0)
    def _with_own():
        pltpu.make_async_copy(bsend.at[0, 0], back.at[0], self_sem.at[1]).wait()
        ref = back.at[pl.ds(0, games - 1)]
        pltpu.make_async_copy(ref, ref, back_recv).wait()

    @pl.when(par != 0)
    def _without_own():
        pltpu.make_async_copy(back, back, back_recv).wait()

    wide = back[...].astype(F32).reshape(games, 2, CAP, half)
    for h in range(2):
        side = wide[:, h].reshape(games * CAP, half).astype(BF16)
        ig[:, h * half:(h + 1) * half] = jnp.dot(taking, side, preferred_element_type=F32).astype(BF16)
    ig_copy = pltpu.make_async_copy(ig, ig_hbm, out_sem.at[1])
    ig_copy.start()

    for c in range(2):

        @pl.when(core == c)
        def _sent():
            for ref, sem in (
                (relay.at[:, pl.ds(0, up - 1 + c)], relay_send),
                (relay.at[:, pl.ds(0, up - c)], fwd_send),
                (relay.at[:, pl.ds(0, up - c)], fwd_send),
            ):
                pltpu.make_async_copy(ref, ref, sem).wait()

    ref = bsend.at[0, pl.ds(0, 2 * ny - 1)]
    pltpu.make_async_copy(ref, ref, fwd_send).wait()

    @pl.when(gathers)
    def _gathered():
        if pieces > 1:
            ref = part.at[:, pl.ds(0, pieces - 1)]
            pltpu.make_async_copy(ref, ref, rs_send).wait()
            ref = mixed.at[:, pl.ds(0, pieces - 1)]
            pltpu.make_async_copy(ref, ref, ag_send).wait()
        pltpu.make_async_copy(swap_out, swap_out, swap_send).wait()
        pltpu.make_async_copy(mixed, mixed, ag_send).wait()

    @pl.when(jnp.logical_not(gathers))
    def _given():
        pltpu.make_async_copy(part, part, rs_send).wait()

    @pl.when(par == 0)
    def _sent_back():
        for ref in (bsend.at[pl.ds(0, ny - 1)], bsend.at[0, pl.ds(0, nz - 1)]):
            pltpu.make_async_copy(ref, ref, back_send).wait()

    ag_copy.wait()
    ig_copy.wait()


def solution(mesh, ny=NY, part_type=BF16, interpret=False):
    nb, nt = mesh.shape["batch"], mesh.shape["tensor"]
    nz = nb // ny

    def body(tokens, cotangent, game_ids, adapters):
        count, features = tokens.shape
        hidden = adapters.shape[2]
        games = nb // 2
        half = features // 2
        np_ = nz // 2
        chunk = nz * CAP
        pieces = nt // 2
        piece = chunk // pieces
        dma = pltpu.SemaphoreType.DMA
        any_ = pl.BlockSpec(memory_space=pl.ANY)
        ig, ag = pl.pallas_call(
            functools.partial(kernel, ny, nz, nt, part_type),
            out_shape=(
                jax.ShapeDtypeStruct((count, features), BF16),
                jax.ShapeDtypeStruct((features, hidden), BF16),
            ),
            in_specs=[pl.BlockSpec(memory_space=pltpu.VMEM), any_, any_, any_],
            out_specs=(any_, any_),
            scratch_shapes=[
                pltpu.VMEM((count, features), BF16),
                pltpu.VMEM((count, features), BF16),
                pltpu.VMEM((features, hidden), BF16),
                pltpu.VMEM((games, 2, 16, half), BF16),
                pltpu.VMEM((ny, np_ // 2, 2, 16, half), BF16),
                pltpu.VMEM((ny, nz, 16, half), BF16),
                pltpu.VMEM((ny, chunk, features), BF16),
                pltpu.VMEM((ny, pieces, piece, hidden), part_type),
                pltpu.VMEM((ny, nt - 1, piece, hidden), part_type),
                pltpu.VMEM((ny, piece, hidden), BF16),
                pltpu.VMEM((ny, piece, hidden), BF16),
                pltpu.VMEM((piece, hidden), F32),
                pltpu.VMEM((ny, pieces, piece, hidden), BF16),
                pltpu.VMEM((ny, nz, 16, half), BF16),
                pltpu.VMEM((games, 16, half), BF16),
                pltpu.VMEM((count, features), BF16),
                pltpu.VMEM((features, hidden), BF16),
                dma((3,)), dma((2,)), dma((2,)),
                dma, dma((ny,)),
                dma, dma((ny,)),
                dma, dma((ny,)),
                dma, dma((ny,)),
                dma, dma((ny,)),
                dma, dma,
            ],
            compiler_params=pltpu.CompilerParams(
                collective_id=0, has_side_effects=True, vmem_limit_bytes=48 << 20
            ),
            interpret=interpret,
        )(game_ids.reshape(1, count), tokens, cotangent, adapters.reshape(features, hidden))
        return ig, ag.reshape(1, features, hidden)

    return jax.shard_map(
        body,
        mesh=mesh,
        in_specs=(P("batch", "tensor"), P("batch", "tensor"), P("batch"), P("batch", "tensor", None)),
        out_specs=(P("batch", "tensor"), P("batch", "tensor", None)),
        check_vma=False,
    )
```

```python
import functools

import jax
import jax.numpy as jnp
from jax import lax
from jax.experimental import pallas as pl
from jax.experimental.pallas import tpu as pltpu
from jax.sharding import PartitionSpec as P

MESH = pl.DeviceIdType.MESH
GELU_SCALE = 0.7978845608028654
GELU_CUBIC = 0.044715
CAP = 8
AHEAD = 2
NY = 4
F32 = jnp.float32
BF16 = jnp.bfloat16


def smooth_gate(v):
    inner = GELU_SCALE * (v + GELU_CUBIC * v * v * v)
    return 0.5 * v * (1.0 + jnp.tanh(inner))


def gate_slope(v):
    inner = GELU_SCALE * (v + GELU_CUBIC * v * v * v)
    tangent = jnp.tanh(inner)
    return 0.5 * (1.0 + tangent) + 0.5 * v * (1.0 - tangent * tangent) * GELU_SCALE * (
        1.0 + 3.0 * GELU_CUBIC * v * v
    )


def kernel(
    ny, nz, nt, part_type,
    ids_ref, tok_hbm, cot_hbm, w_hbm,
    ig_hbm, ag_hbm,
    tok, cot, w, sends, relay, arrived, rows, pair_out, pair_in, own, part, summands, swap_out, swap_in, slope, mixed, bsend, back, ig, ag,
    in_sem, out_sem, self_sem, relay_send, relay_recv, fwd_send, fwd_recv, pair_send, pair_recv, rs_send, rs_recv, pass_send, swap_send, swap_recv, ag_send, ag_recv,
    back_send, back_recv,
):
    nb = ny * nz
    np_ = nz // 2
    me = lax.axis_index("batch")
    t = lax.axis_index("tensor")
    y, z = me // nz, me % nz
    p, par = z // 2, z % 2
    core, x = t % 2, t // 2
    sibling = t + 1 - 2 * core
    gather_core = 1 - par
    gathers = core == gather_core
    count, features = tok.shape
    hidden = w.shape[1]
    half = features // 2
    games = nb // 2
    chunk = nz * CAP
    pieces = nt // 2
    piece = chunk // pieces
    up = np_ // 2

    copies = [
        pltpu.make_async_copy(a, b, in_sem.at[i])
        for i, (a, b) in enumerate(((tok_hbm, tok), (cot_hbm, cot), (w_hbm, w)))
    ]
    for c in copies:
        c.start()

    barrier = pltpu.get_barrier_semaphore()

    def greet_batch(k, _):
        pl.semaphore_signal(barrier, inc=1, device_id={"batch": (me + k) % nb}, device_id_type=MESH)
        return _

    def greet_tensor(k, _):
        pl.semaphore_signal(barrier, inc=1, device_id={"tensor": (t + k) % nt}, device_id_type=MESH)
        return _

    lax.fori_loop(1, nb, greet_batch, 0)
    lax.fori_loop(1, nt, greet_tensor, 0)

    ids = ids_ref[...]
    member = (lax.broadcasted_iota(jnp.int32, (games, count), 0) == ids).astype(F32)
    earlier = (
        lax.broadcasted_iota(jnp.int32, (count, count), 0) < lax.broadcasted_iota(jnp.int32, (count, count), 1)
    ).astype(F32)
    before = jnp.dot(member.astype(BF16), earlier.astype(BF16), preferred_element_type=F32)
    position = jnp.sum(before * member, axis=0, keepdims=True).astype(jnp.int32)
    gy, gp = ids // np_, ids % np_
    target = (((gy - y + ny) % ny) * np_ + (gp - p + np_) % np_) * CAP + position

    place = lax.broadcasted_iota(jnp.int32, (2 * games * CAP, count), 0)
    slot = (place // 16) * CAP + place % CAP
    placing = (slot == target).astype(BF16)
    on_left = lax.broadcasted_iota(jnp.int32, (2 * games * CAP, half), 0) % 16 < 8
    for q in range(2):
        copies[q].wait()
        src = (tok, cot)[q]
        left = jnp.dot(placing, src[:, :half], preferred_element_type=F32)
        right = jnp.dot(placing, src[:, half:], preferred_element_type=F32)
        sends[:, q] = jnp.where(on_left, left, right).astype(BF16).reshape(games, 16, half)

    pl.semaphore_wait(barrier, nb - 1 + nt - 1)

    own_block = pltpu.make_async_copy(sends.at[0, par], arrived.at[0, par], self_sem.at[0])
    own_block.start()

    def relay_part(dy, for_core):
        first, number = ((1, up), (up + 1, up - 1))[for_core]
        return sends.at[pl.ds(dy * np_ + first, number)], relay.at[dy, pl.ds(0, number)]

    for c in range(2):

        @pl.when(core != c)
        def _hand_over():
            def hand_over(dy, _):
                src, dst = relay_part(dy, c)
                pltpu.make_async_remote_copy(
                    src_ref=src,
                    dst_ref=dst,
                    send_sem=relay_send,
                    recv_sem=relay_recv.at[dy],
                    device_id={"tensor": sibling},
                    device_id_type=MESH,
                ).start()
                return _

            lax.fori_loop(0, ny, hand_over, 0)

    def send_block(src, dy, dp, q, tensor):
        far = ((y + dy) % ny) * nz + 2 * ((p + dp) % np_) + q
        pltpu.make_async_remote_copy(
            src_ref=src,
            dst_ref=arrived.at[dy, 2 * dp + par],
            send_sem=fwd_send,
            recv_sem=fwd_recv.at[dy],
            device_id={"batch": far, "tensor": tensor},
            device_id_type=MESH,
        ).start()

    def send_forward(dy, _):
        for c in range(2):

            @pl.when(core == c)
            def _own_way():
                number = up - c

                def own(i, _):
                    dp = up + 1 + i if c else up - i
                    for q in range(2):
                        send_block(sends.at[dy * np_ + dp, q], dy, dp, q, t)
                    return _

                def relayed(i, _):
                    dp = up + 1 + i if c else up - i
                    for q in range(2):
                        send_block(relay.at[dy, i if c else up - 1 - i, q], dy, dp, q, sibling)
                    return _

                lax.fori_loop(0, number, own, 0)
                _, ref = relay_part(dy, c)
                pltpu.make_async_copy(ref, ref, relay_recv.at[dy]).wait()
                lax.fori_loop(0, number, relayed, 0)

        send_block(sends.at[dy * np_, 1 - par], dy, 0, 1 - par, t)

        @pl.when(dy != 0)
        def _straight():
            send_block(sends.at[dy * np_, par], dy, 0, par, t)

        return _

    lax.fori_loop(0, AHEAD, send_forward, 0)
    copies[2].wait()

    def arrive(c):
        @pl.when(c == 0)
        def _first():
            own_block.wait()
            ref = arrived.at[0, pl.ds(0, nz - 1)]
            pltpu.make_async_copy(ref, ref, fwd_recv.at[0]).wait()

        @pl.when(c != 0)
        def _later():
            ref = arrived.at[c]
            pltpu.make_async_copy(ref, ref, fwd_recv.at[c]).wait()

        @pl.when(c + AHEAD < ny)
        def _next():
            send_forward(c + AHEAD, 0)

        wide = arrived[c].astype(F32).reshape(nz, 2, CAP, half)
        rows[c, :, :half] = wide[:, 0].reshape(chunk, half).astype(BF16)
        rows[c, :, half:] = wide[:, 1].reshape(chunk, half).astype(BF16)

        product = jnp.dot(rows[c], w[...], preferred_element_type=F32).reshape(pieces, piece, hidden)

        @pl.when(jnp.logical_not(gathers))
        def _give():
            pair_out[c] = product
            pltpu.make_async_remote_copy(
                src_ref=pair_out.at[c],
                dst_ref=pair_in.at[c],
                send_sem=pair_send,
                recv_sem=pair_recv.at[c],
                device_id={"tensor": sibling},
                device_id_type=MESH,
            ).start()

        @pl.when(gathers)
        def _take():
            pair_out[c] = product
            ref = pair_in.at[c]
            pltpu.make_async_copy(ref, ref, pair_recv.at[c]).wait()
            part[c] = (pair_out[c] + pair_in[c]).astype(part_type)
            own[...] = pair_out[c, x] + pair_in[c, x]

            def send_part(k, _):
                to = (x + k) % pieces
                pltpu.make_async_remote_copy(
                    src_ref=part.at[c, to],
                    dst_ref=summands.at[c, pieces - k - 1],
                    send_sem=rs_send,
                    recv_sem=rs_recv.at[c],
                    device_id={"tensor": 2 * to + gather_core},
                    device_id_type=MESH,
                ).start()
                return _

            lax.fori_loop(1, pieces, send_part, 0)

    def swap_copy(c):
        return pltpu.make_async_remote_copy(
            src_ref=swap_out.at[c],
            dst_ref=swap_in.at[c],
            send_sem=swap_send,
            recv_sem=swap_recv.at[c],
            device_id={"batch": me + 1 - 2 * par, "tensor": 2 * x + par},
            device_id_type=MESH,
        )

    def combine(c):
        total = own[...]
        if pieces > 1:
            ref = summands.at[c]
            pltpu.make_async_copy(ref, ref, rs_recv.at[c]).wait()
            for k in range(pieces - 1):
                total = total + summands[c, k].astype(F32)
        swap_out[c] = jnp.where(par == 0, smooth_gate(total), total).astype(BF16)
        swap_copy(c).start()
        slope[...] = jnp.where(par == 0, gate_slope(total), 1.0)

    def spread(c):
        swap_copy(c).wait_recv()
        mixed[c, x] = (swap_in[c].astype(F32) * slope[...]).astype(BF16)

        def send_mixed(k, _):
            pltpu.make_async_remote_copy(
                src_ref=mixed.at[c, x],
                dst_ref=mixed.at[c, x],
                send_sem=ag_send,
                recv_sem=ag_recv.at[c],
                device_id={"tensor": 2 * ((x + k) % pieces) + gather_core},
                device_id_type=MESH,
            ).start()
            return _

        lax.fori_loop(1, pieces, send_mixed, 0)

    def give_back(c):
        @pl.when(gathers)
        def _pass_on():
            if pieces > 1:
                ref = mixed.at[c, pl.ds(0, pieces - 1)]
                pltpu.make_async_copy(ref, ref, ag_recv.at[c]).wait()
            pltpu.make_async_remote_copy(
                src_ref=mixed.at[c],
                dst_ref=mixed.at[c],
                send_sem=pass_send,
                recv_sem=ag_recv.at[c],
                device_id={"tensor": sibling},
                device_id_type=MESH,
            ).start()

        @pl.when(jnp.logical_not(gathers))
        def _passed():
            ref = mixed.at[c]
            pltpu.make_async_copy(ref, ref, ag_recv.at[c]).wait()

        @pl.when(par == 0)
        def _input_gradient():
            grad = lax.dot_general(
                mixed[c].reshape(chunk, hidden), w[...], (((1,), (1,)), ((), ())), preferred_element_type=F32
            )
            pair = jnp.stack(
                [grad[:, :half].reshape(nz, CAP, half), grad[:, half:].reshape(nz, CAP, half)], axis=1
            )
            bsend[c] = pair.reshape(nz, 16, half).astype(BF16)

    def start_back(c):
        @pl.when(par == 0)
        def _start():
            def send_back(j, _):
                dp, from_par = j // 2, j % 2
                far = ((y - c + ny) % ny) * nz + 2 * ((p - dp + np_) % np_) + from_par

                @pl.when(far != me)
                def _send():
                    pltpu.make_async_remote_copy(
                        src_ref=bsend.at[c, j],
                        dst_ref=back.at[c * np_ + dp],
                        send_sem=back_send,
                        recv_sem=back_recv,
                        device_id={"batch": far},
                        device_id_type=MESH,
                    ).start()

                @pl.when(far == me)
                def _keep():
                    pltpu.make_async_copy(bsend.at[0, 0], back.at[0], self_sem.at[1]).start()

                return _

            lax.fori_loop(0, nz, send_back, 0)

    def per_chunk(k, _):
        @pl.when(k < ny)
        def _arrive():
            arrive(k)

        @pl.when(k > 0)
        def _give_back():
            give_back(k - 1)

        @pl.when((k < ny) & gathers)
        def _combine():
            combine(k)

        @pl.when(k > 0)
        def _start_back():
            start_back(k - 1)

        @pl.when((k < ny) & gathers)
        def _spread():
            spread(k)

        return _

    lax.fori_loop(0, ny + 1, per_chunk, 0)

    every = ny * chunk

    product = lax.dot_general(
        rows[...].reshape(every, features), mixed[...].reshape(every, hidden), (((0,), (0,)), ((), ())),
        preferred_element_type=F32,
    )
    ag[...] = product.astype(BF16)
    ag_copy = pltpu.make_async_copy(ag, ag_hbm, out_sem.at[0])
    ag_copy.start()

    eye = lax.broadcasted_iota(jnp.int32, (count, count), 0) == lax.broadcasted_iota(jnp.int32, (count, count), 1)
    target_column = jnp.sum(jnp.where(eye, target, 0), axis=1, keepdims=True)
    taking = (lax.broadcasted_iota(jnp.int32, (count, games * CAP), 1) == target_column).astype(BF16)

    @pl.when(par == 0)
    def _with_own():
        pltpu.make_async_copy(bsend.at[0, 0], back.at[0], self_sem.at[1]).wait()
        ref = back.at[pl.ds(0, games - 1)]
        pltpu.make_async_copy(ref, ref, back_recv).wait()

    @pl.when(par != 0)
    def _without_own():
        pltpu.make_async_copy(back, back, back_recv).wait()

    wide = back[...].astype(F32).reshape(games, 2, CAP, half)
    for h in range(2):
        side = wide[:, h].reshape(games * CAP, half).astype(BF16)
        ig[:, h * half:(h + 1) * half] = jnp.dot(taking, side, preferred_element_type=F32).astype(BF16)
    ig_copy = pltpu.make_async_copy(ig, ig_hbm, out_sem.at[1])
    ig_copy.start()

    for c in range(2):

        @pl.when(core == c)
        def _sent():
            for ref, sem in (
                (relay.at[:, pl.ds(0, up - 1 + c)], relay_send),
                (relay.at[:, pl.ds(0, up - c)], fwd_send),
                (relay.at[:, pl.ds(0, up - c)], fwd_send),
            ):
                pltpu.make_async_copy(ref, ref, sem).wait()

    ref = bsend.at[0, pl.ds(0, 2 * ny - 1)]
    pltpu.make_async_copy(ref, ref, fwd_send).wait()

    @pl.when(gathers)
    def _gathered():
        if pieces > 1:
            ref = part.at[:, pl.ds(0, pieces - 1)]
            pltpu.make_async_copy(ref, ref, rs_send).wait()
            ref = mixed.at[:, pl.ds(0, pieces - 1)]
            pltpu.make_async_copy(ref, ref, ag_send).wait()
        pltpu.make_async_copy(swap_out, swap_out, swap_send).wait()
        pltpu.make_async_copy(mixed, mixed, pass_send).wait()

    @pl.when(jnp.logical_not(gathers))
    def _given():
        pltpu.make_async_copy(pair_out, pair_out, pair_send).wait()

    @pl.when(par == 0)
    def _sent_back():
        for ref in (bsend.at[pl.ds(0, ny - 1)], bsend.at[0, pl.ds(0, nz - 1)]):
            pltpu.make_async_copy(ref, ref, back_send).wait()

    ag_copy.wait()
    ig_copy.wait()


def solution(mesh, ny=NY, part_type=BF16, interpret=False):
    nb, nt = mesh.shape["batch"], mesh.shape["tensor"]
    nz = nb // ny

    def body(tokens, cotangent, game_ids, adapters):
        count, features = tokens.shape
        hidden = adapters.shape[2]
        games = nb // 2
        half = features // 2
        np_ = nz // 2
        chunk = nz * CAP
        pieces = nt // 2
        piece = chunk // pieces
        dma = pltpu.SemaphoreType.DMA
        any_ = pl.BlockSpec(memory_space=pl.ANY)
        ig, ag = pl.pallas_call(
            functools.partial(kernel, ny, nz, nt, part_type),
            out_shape=(
                jax.ShapeDtypeStruct((count, features), BF16),
                jax.ShapeDtypeStruct((features, hidden), BF16),
            ),
            in_specs=[pl.BlockSpec(memory_space=pltpu.VMEM), any_, any_, any_],
            out_specs=(any_, any_),
            scratch_shapes=[
                pltpu.VMEM((count, features), BF16),
                pltpu.VMEM((count, features), BF16),
                pltpu.VMEM((features, hidden), BF16),
                pltpu.VMEM((games, 2, 16, half), BF16),
                pltpu.VMEM((ny, np_ // 2, 2, 16, half), BF16),
                pltpu.VMEM((ny, nz, 16, half), BF16),
                pltpu.VMEM((ny, chunk, features), BF16),
                pltpu.VMEM((ny, pieces, piece, hidden), F32),
                pltpu.VMEM((ny, pieces, piece, hidden), F32),
                pltpu.VMEM((piece, hidden), F32),
                pltpu.VMEM((ny, pieces, piece, hidden), part_type),
                pltpu.VMEM((ny, max(pieces - 1, 1), piece, hidden), part_type),
                pltpu.VMEM((ny, piece, hidden), BF16),
                pltpu.VMEM((ny, piece, hidden), BF16),
                pltpu.VMEM((piece, hidden), F32),
                pltpu.VMEM((ny, pieces, piece, hidden), BF16),
                pltpu.VMEM((ny, nz, 16, half), BF16),
                pltpu.VMEM((games, 16, half), BF16),
                pltpu.VMEM((count, features), BF16),
                pltpu.VMEM((features, hidden), BF16),
                dma((3,)), dma((2,)), dma((2,)),
                dma, dma((ny,)),
                dma, dma((ny,)),
                dma, dma((ny,)),
                dma, dma((ny,)),
                dma,
                dma, dma((ny,)),
                dma, dma((ny,)),
                dma, dma,
            ],
            compiler_params=pltpu.CompilerParams(
                collective_id=0, has_side_effects=True, vmem_limit_bytes=48 << 20
            ),
            interpret=interpret,
        )(game_ids.reshape(1, count), tokens, cotangent, adapters.reshape(features, hidden))
        return ig, ag.reshape(1, features, hidden)

    return jax.shard_map(
        body,
        mesh=mesh,
        in_specs=(P("batch", "tensor"), P("batch", "tensor"), P("batch"), P("batch", "tensor", None)),
        out_specs=(P("batch", "tensor"), P("batch", "tensor", None)),
        check_vma=False,
    )
```

```python
import functools

import jax
import jax.numpy as jnp
from jax import lax
from jax.experimental import pallas as pl
from jax.experimental.pallas import tpu as pltpu
from jax.sharding import PartitionSpec as P

MESH = pl.DeviceIdType.MESH
GELU_SCALE = 0.7978845608028654
GELU_CUBIC = 0.044715
CAP = 8
AHEAD = 2
NY = 4
F32 = jnp.float32
BF16 = jnp.bfloat16


def smooth_gate(v):
    inner = GELU_SCALE * (v + GELU_CUBIC * v * v * v)
    return 0.5 * v * (1.0 + jnp.tanh(inner))


def gate_slope(v):
    inner = GELU_SCALE * (v + GELU_CUBIC * v * v * v)
    tangent = jnp.tanh(inner)
    return 0.5 * (1.0 + tangent) + 0.5 * v * (1.0 - tangent * tangent) * GELU_SCALE * (
        1.0 + 3.0 * GELU_CUBIC * v * v
    )


def kernel(
    ny, nz, nt, part_type,
    ids_ref, tok_hbm, cot_hbm, w_hbm,
    ig_hbm, ag_hbm,
    tok, cot, w, sends, relay, arrived, rows, pair_out, pair_in, own, part, summands, swap_out, swap_in, slope, mixed, bsend, back, ig, ag,
    in_sem, out_sem, self_sem, relay_send, relay_recv, fwd_send, fwd_recv, pair_send, pair_recv, rs_send, rs_recv, pass_send, swap_send, swap_recv, ag_send, ag_recv,
    back_send, back_recv,
):
    nb = ny * nz
    np_ = nz // 2
    me = lax.axis_index("batch")
    t = lax.axis_index("tensor")
    y, z = me // nz, me % nz
    p, par = z // 2, z % 2
    core, x = t % 2, t // 2
    sibling = t + 1 - 2 * core
    gather_core = 1 - par
    gathers = core == gather_core
    count, features = tok.shape
    hidden = w.shape[1]
    half = features // 2
    games = nb // 2
    chunk = nz * CAP
    pieces = nt // 2
    piece = chunk // pieces
    up = np_ // 2

    copies = [
        pltpu.make_async_copy(a, b, in_sem.at[i])
        for i, (a, b) in enumerate(((tok_hbm, tok), (cot_hbm, cot), (w_hbm, w)))
    ]
    for c in copies:
        c.start()

    barrier = pltpu.get_barrier_semaphore()

    def greet_batch(k, _):
        pl.semaphore_signal(barrier, inc=1, device_id={"batch": (me + k) % nb}, device_id_type=MESH)
        return _

    def greet_tensor(k, _):
        pl.semaphore_signal(barrier, inc=1, device_id={"tensor": (t + k) % nt}, device_id_type=MESH)
        return _

    lax.fori_loop(1, nb, greet_batch, 0)
    lax.fori_loop(1, nt, greet_tensor, 0)

    ids = ids_ref[...]
    member = (lax.broadcasted_iota(jnp.int32, (games, count), 0) == ids).astype(F32)
    earlier = (
        lax.broadcasted_iota(jnp.int32, (count, count), 0) < lax.broadcasted_iota(jnp.int32, (count, count), 1)
    ).astype(F32)
    before = jnp.dot(member.astype(BF16), earlier.astype(BF16), preferred_element_type=F32)
    position = jnp.sum(before * member, axis=0, keepdims=True).astype(jnp.int32)
    gy, gp = ids // np_, ids % np_
    target = (((gy - y + ny) % ny) * np_ + (gp - p + np_) % np_) * CAP + position

    place = lax.broadcasted_iota(jnp.int32, (2 * games * CAP, count), 0)
    slot = (place // 16) * CAP + place % CAP
    placing = (slot == target).astype(BF16)
    on_left = lax.broadcasted_iota(jnp.int32, (2 * games * CAP, half), 0) % 16 < 8
    for q in range(2):
        copies[q].wait()
        src = (tok, cot)[q]
        left = jnp.dot(placing, src[:, :half], preferred_element_type=F32)
        right = jnp.dot(placing, src[:, half:], preferred_element_type=F32)
        sends[:, q] = jnp.where(on_left, left, right).astype(BF16).reshape(games, 16, half)

    pl.semaphore_wait(barrier, nb - 1 + nt - 1)

    own_block = pltpu.make_async_copy(sends.at[0, par], arrived.at[0, par], self_sem.at[0])
    own_block.start()

    def relay_part(dy, for_core):
        first, number = ((1, up), (up + 1, up - 1))[for_core]
        return sends.at[pl.ds(dy * np_ + first, number)], relay.at[dy, pl.ds(0, number)]

    for c in range(2):

        @pl.when(core != c)
        def _hand_over():
            def hand_over(dy, _):
                src, dst = relay_part(dy, c)
                pltpu.make_async_remote_copy(
                    src_ref=src,
                    dst_ref=dst,
                    send_sem=relay_send,
                    recv_sem=relay_recv.at[dy],
                    device_id={"tensor": sibling},
                    device_id_type=MESH,
                ).start()
                return _

            lax.fori_loop(0, ny, hand_over, 0)

    def send_block(src, dy, dp, q, tensor):
        far = ((y + dy) % ny) * nz + 2 * ((p + dp) % np_) + q
        pltpu.make_async_remote_copy(
            src_ref=src,
            dst_ref=arrived.at[dy, 2 * dp + par],
            send_sem=fwd_send,
            recv_sem=fwd_recv.at[dy],
            device_id={"batch": far, "tensor": tensor},
            device_id_type=MESH,
        ).start()

    def send_forward(dy, _):
        for c in range(2):

            @pl.when(core == c)
            def _own_way():
                number = up - c

                def own(i, _):
                    dp = up + 1 + i if c else up - i
                    for q in range(2):
                        send_block(sends.at[dy * np_ + dp, q], dy, dp, q, t)
                    return _

                def relayed(i, _):
                    dp = up + 1 + i if c else up - i
                    for q in range(2):
                        send_block(relay.at[dy, i if c else up - 1 - i, q], dy, dp, q, sibling)
                    return _

                lax.fori_loop(0, number, own, 0)
                _, ref = relay_part(dy, c)
                pltpu.make_async_copy(ref, ref, relay_recv.at[dy]).wait()
                lax.fori_loop(0, number, relayed, 0)

        send_block(sends.at[dy * np_, 1 - par], dy, 0, 1 - par, t)

        @pl.when(dy != 0)
        def _straight():
            send_block(sends.at[dy * np_, par], dy, 0, par, t)

        return _

    lax.fori_loop(0, AHEAD, send_forward, 0)
    copies[2].wait()

    def arrive(c):
        @pl.when(c == 0)
        def _first():
            own_block.wait()
            ref = arrived.at[0, pl.ds(0, nz - 1)]
            pltpu.make_async_copy(ref, ref, fwd_recv.at[0]).wait()

        @pl.when(c != 0)
        def _later():
            ref = arrived.at[c]
            pltpu.make_async_copy(ref, ref, fwd_recv.at[c]).wait()

        wide = arrived[c].astype(F32).reshape(nz, 2, CAP, half)
        rows[c, :, :half] = wide[:, 0].reshape(chunk, half).astype(BF16)
        rows[c, :, half:] = wide[:, 1].reshape(chunk, half).astype(BF16)

        for h in range(2):
            cols = slice(h * (hidden // 2), (h + 1) * (hidden // 2))
            product = jnp.dot(rows[c], w[:, cols], preferred_element_type=F32)
            pair_out[c, h] = product.reshape(pieces, piece, hidden // 2)

            @pl.when(jnp.logical_not(gathers))
            def _give():
                pltpu.make_async_remote_copy(
                    src_ref=pair_out.at[c, h],
                    dst_ref=pair_in.at[c, h],
                    send_sem=pair_send,
                    recv_sem=pair_recv.at[c, h],
                    device_id={"tensor": sibling},
                    device_id_type=MESH,
                ).start()

        @pl.when(gathers)
        def _take():
            for h in range(2):
                cols = slice(h * (hidden // 2), (h + 1) * (hidden // 2))
                ref = pair_in.at[c, h]
                pltpu.make_async_copy(ref, ref, pair_recv.at[c, h]).wait()
                part[c, :, :, cols] = (pair_out[c, h] + pair_in[c, h]).astype(part_type)
                own[:, cols] = pair_out[c, h, x] + pair_in[c, h, x]

            def send_part(k, _):
                to = (x + k) % pieces
                pltpu.make_async_remote_copy(
                    src_ref=part.at[c, to],
                    dst_ref=summands.at[c, pieces - k - 1],
                    send_sem=rs_send,
                    recv_sem=rs_recv.at[c],
                    device_id={"tensor": 2 * to + gather_core},
                    device_id_type=MESH,
                ).start()
                return _

            lax.fori_loop(1, pieces, send_part, 0)

        @pl.when(c + AHEAD < ny)
        def _next():
            send_forward(c + AHEAD, 0)

    def swap_copy(c):
        return pltpu.make_async_remote_copy(
            src_ref=swap_out.at[c],
            dst_ref=swap_in.at[c],
            send_sem=swap_send,
            recv_sem=swap_recv.at[c],
            device_id={"batch": me + 1 - 2 * par, "tensor": 2 * x + par},
            device_id_type=MESH,
        )

    def combine(c):
        total = own[...]
        if pieces > 1:
            ref = summands.at[c]
            pltpu.make_async_copy(ref, ref, rs_recv.at[c]).wait()
            for k in range(pieces - 1):
                total = total + summands[c, k].astype(F32)
        swap_out[c] = jnp.where(par == 0, smooth_gate(total), total).astype(BF16)
        swap_copy(c).start()
        slope[...] = jnp.where(par == 0, gate_slope(total), 1.0)

    def spread(c):
        swap_copy(c).wait_recv()
        mixed[c, x] = (swap_in[c].astype(F32) * slope[...]).astype(BF16)

        def send_mixed(k, _):
            pltpu.make_async_remote_copy(
                src_ref=mixed.at[c, x],
                dst_ref=mixed.at[c, x],
                send_sem=ag_send,
                recv_sem=ag_recv.at[c],
                device_id={"tensor": 2 * ((x + k) % pieces) + gather_core},
                device_id_type=MESH,
            ).start()
            return _

        lax.fori_loop(1, pieces, send_mixed, 0)

    def give_back(c):
        @pl.when(gathers)
        def _pass_on():
            if pieces > 1:
                ref = mixed.at[c, pl.ds(0, pieces - 1)]
                pltpu.make_async_copy(ref, ref, ag_recv.at[c]).wait()
            pltpu.make_async_remote_copy(
                src_ref=mixed.at[c],
                dst_ref=mixed.at[c],
                send_sem=pass_send,
                recv_sem=ag_recv.at[c],
                device_id={"tensor": sibling},
                device_id_type=MESH,
            ).start()

        @pl.when(jnp.logical_not(gathers))
        def _passed():
            ref = mixed.at[c]
            pltpu.make_async_copy(ref, ref, ag_recv.at[c]).wait()

    def gradient(c):
        @pl.when(par == 0)
        def _input_gradient():
            grad = lax.dot_general(
                mixed[c].reshape(chunk, hidden), w[...], (((1,), (1,)), ((), ())), preferred_element_type=F32
            )
            pair = jnp.stack(
                [grad[:, :half].reshape(nz, CAP, half), grad[:, half:].reshape(nz, CAP, half)], axis=1
            )
            bsend[c] = pair.reshape(nz, 16, half).astype(BF16)

    def start_back(c):
        @pl.when(par == 0)
        def _start():
            def send_back(j, _):
                dp, from_par = j // 2, j % 2
                far = ((y - c + ny) % ny) * nz + 2 * ((p - dp + np_) % np_) + from_par

                @pl.when(far != me)
                def _send():
                    pltpu.make_async_remote_copy(
                        src_ref=bsend.at[c, j],
                        dst_ref=back.at[c * np_ + dp],
                        send_sem=back_send,
                        recv_sem=back_recv,
                        device_id={"batch": far},
                        device_id_type=MESH,
                    ).start()

                @pl.when(far == me)
                def _keep():
                    pltpu.make_async_copy(bsend.at[0, 0], back.at[0], self_sem.at[1]).start()

                return _

            lax.fori_loop(0, nz, send_back, 0)

    def per_chunk(k, _):
        @pl.when(k < ny)
        def _arrive():
            arrive(k)

        @pl.when(k > 0)
        def _give_back():
            give_back(k - 1)

        @pl.when((k < ny) & gathers)
        def _combine():
            combine(k)

        @pl.when(k > 0)
        def _start_back():
            gradient(k - 1)
            start_back(k - 1)

        @pl.when((k < ny) & gathers)
        def _spread():
            spread(k)

        return _

    lax.fori_loop(0, ny + 1, per_chunk, 0)

    every = ny * chunk

    product = lax.dot_general(
        rows[...].reshape(every, features), mixed[...].reshape(every, hidden), (((0,), (0,)), ((), ())),
        preferred_element_type=F32,
    )
    ag[...] = product.astype(BF16)
    ag_copy = pltpu.make_async_copy(ag, ag_hbm, out_sem.at[0])
    ag_copy.start()

    eye = lax.broadcasted_iota(jnp.int32, (count, count), 0) == lax.broadcasted_iota(jnp.int32, (count, count), 1)
    target_column = jnp.sum(jnp.where(eye, target, 0), axis=1, keepdims=True)
    taking = (lax.broadcasted_iota(jnp.int32, (count, games * CAP), 1) == target_column).astype(BF16)

    @pl.when(par == 0)
    def _with_own():
        pltpu.make_async_copy(bsend.at[0, 0], back.at[0], self_sem.at[1]).wait()
        ref = back.at[pl.ds(0, games - 1)]
        pltpu.make_async_copy(ref, ref, back_recv).wait()

    @pl.when(par != 0)
    def _without_own():
        pltpu.make_async_copy(back, back, back_recv).wait()

    wide = back[...].astype(F32).reshape(games, 2, CAP, half)
    for h in range(2):
        side = wide[:, h].reshape(games * CAP, half).astype(BF16)
        ig[:, h * half:(h + 1) * half] = jnp.dot(taking, side, preferred_element_type=F32).astype(BF16)
    ig_copy = pltpu.make_async_copy(ig, ig_hbm, out_sem.at[1])
    ig_copy.start()

    for c in range(2):

        @pl.when(core == c)
        def _sent():
            for ref, sem in (
                (relay.at[:, pl.ds(0, up - 1 + c)], relay_send),
                (relay.at[:, pl.ds(0, up - c)], fwd_send),
                (relay.at[:, pl.ds(0, up - c)], fwd_send),
            ):
                pltpu.make_async_copy(ref, ref, sem).wait()

    ref = bsend.at[0, pl.ds(0, 2 * ny - 1)]
    pltpu.make_async_copy(ref, ref, fwd_send).wait()

    @pl.when(gathers)
    def _gathered():
        if pieces > 1:
            ref = part.at[:, pl.ds(0, pieces - 1)]
            pltpu.make_async_copy(ref, ref, rs_send).wait()
            ref = mixed.at[:, pl.ds(0, pieces - 1)]
            pltpu.make_async_copy(ref, ref, ag_send).wait()
        pltpu.make_async_copy(swap_out, swap_out, swap_send).wait()
        pltpu.make_async_copy(mixed, mixed, pass_send).wait()

    @pl.when(jnp.logical_not(gathers))
    def _given():
        pltpu.make_async_copy(pair_out, pair_out, pair_send).wait()

    @pl.when(par == 0)
    def _sent_back():
        for ref in (bsend.at[pl.ds(0, ny - 1)], bsend.at[0, pl.ds(0, nz - 1)]):
            pltpu.make_async_copy(ref, ref, back_send).wait()

    ag_copy.wait()
    ig_copy.wait()


def solution(mesh, ny=NY, part_type=BF16, interpret=False):
    nb, nt = mesh.shape["batch"], mesh.shape["tensor"]
    nz = nb // ny

    def body(tokens, cotangent, game_ids, adapters):
        count, features = tokens.shape
        hidden = adapters.shape[2]
        games = nb // 2
        half = features // 2
        np_ = nz // 2
        chunk = nz * CAP
        pieces = nt // 2
        piece = chunk // pieces
        dma = pltpu.SemaphoreType.DMA
        any_ = pl.BlockSpec(memory_space=pl.ANY)
        ig, ag = pl.pallas_call(
            functools.partial(kernel, ny, nz, nt, part_type),
            out_shape=(
                jax.ShapeDtypeStruct((count, features), BF16),
                jax.ShapeDtypeStruct((features, hidden), BF16),
            ),
            in_specs=[pl.BlockSpec(memory_space=pltpu.VMEM), any_, any_, any_],
            out_specs=(any_, any_),
            scratch_shapes=[
                pltpu.VMEM((count, features), BF16),
                pltpu.VMEM((count, features), BF16),
                pltpu.VMEM((features, hidden), BF16),
                pltpu.VMEM((games, 2, 16, half), BF16),
                pltpu.VMEM((ny, np_ // 2, 2, 16, half), BF16),
                pltpu.VMEM((ny, nz, 16, half), BF16),
                pltpu.VMEM((ny, chunk, features), BF16),
                pltpu.VMEM((ny, 2, pieces, piece, hidden // 2), F32),
                pltpu.VMEM((ny, 2, pieces, piece, hidden // 2), F32),
                pltpu.VMEM((piece, hidden), F32),
                pltpu.VMEM((ny, pieces, piece, hidden), part_type),
                pltpu.VMEM((ny, max(pieces - 1, 1), piece, hidden), part_type),
                pltpu.VMEM((ny, piece, hidden), BF16),
                pltpu.VMEM((ny, piece, hidden), BF16),
                pltpu.VMEM((piece, hidden), F32),
                pltpu.VMEM((ny, pieces, piece, hidden), BF16),
                pltpu.VMEM((ny, nz, 16, half), BF16),
                pltpu.VMEM((games, 16, half), BF16),
                pltpu.VMEM((count, features), BF16),
                pltpu.VMEM((features, hidden), BF16),
                dma((3,)), dma((2,)), dma((2,)),
                dma, dma((ny,)),
                dma, dma((ny,)),
                dma, dma((ny, 2)),
                dma, dma((ny,)),
                dma,
                dma, dma((ny,)),
                dma, dma((ny,)),
                dma, dma,
            ],
            compiler_params=pltpu.CompilerParams(
                collective_id=0, has_side_effects=True, vmem_limit_bytes=48 << 20
            ),
            interpret=interpret,
        )(game_ids.reshape(1, count), tokens, cotangent, adapters.reshape(features, hidden))
        return ig, ag.reshape(1, features, hidden)

    return jax.shard_map(
        body,
        mesh=mesh,
        in_specs=(P("batch", "tensor"), P("batch", "tensor"), P("batch"), P("batch", "tensor", None)),
        out_specs=(P("batch", "tensor"), P("batch", "tensor", None)),
        check_vma=False,
    )
```
